32 devices in a mesh: strip: 4 (over y, x), along: 8 (over z, core).
Axes of the slice: x: 2, y: 2, z: 4, core: 2. Of those that a mesh axis runs over, the one named last changes fastest.
Arguments:
- images: float32 [256, 4096], P('strip', 'along'), may hold values from 0 to 255
- offsets: int32 [4, 8, 2], P('strip', 'along'), may hold values from 0 to 31
Outputs:
- matches: float32 [8, 256, 4096], P(None, 'strip', 'along')
The draws below stay inside these ranges and needn't reach their ends.
All inputs are finite; a program needn't handle non-finite values.
Results may differ from the reference program's by a relative error of at most 0.000063.
Values sent between devices are 32-bit elements; how exact they have to be, the bound alone decides.
No kernel may reach another device: no remote copies, remote signals or barrier semaphores. Data moves between devices by JAX's collectives and lax.ppermute only.
A program may use at most 64 MiB of HBM per device.

```python
import jax
import jax.numpy as jnp
from jax import lax

ROWS = 64
COLS = 512
DISP = 16
NROWS = 256
NCOLS = 4096
N_STRIP = 4
N_ALONG = 8


def touch_ends(drawn, rng, low, largest):
    shape = drawn.shape
    spot = [jax.random.randint(jax.random.fold_in(rng, axis), (), 0, shape[axis]) for axis in range(len(shape))]
    drawn = drawn.at[tuple(spot)].set(low)
    longest = shape.index(max(shape))
    spot[longest] = (spot[longest] + 1) % shape[longest]
    return drawn.at[tuple(spot)].set(largest)


def shard_levels(stream_key, shape, split, smallest, largest):
    def one(dim, shards_of):
        heights = jax.random.uniform(jax.random.fold_in(jax.random.fold_in(stream_key, 6), dim), (shards_of,), jnp.float32, smallest / len(split), largest / len(split))
        return jnp.repeat(jnp.exp(heights), shape[dim] // shards_of).reshape((-1,) + (1,) * (len(shape) - dim - 1))

    loudness = one(*split[0])
    for cut in split[1:]:
        loudness = loudness * one(*cut)
    return loudness


def setup_inputs(seed: int = 0) -> dict:
    key_list = jax.random.split(jax.random.key(seed), 3)
    return {
        "images": jnp.clip(255.0 * jax.random.uniform(key_list[0], (NROWS, NCOLS), jnp.float32) ** shard_levels(key_list[0], (NROWS, NCOLS), ((0, 4), (1, 8)), -0.2, 0.2), 0.0, 255.0),
        "offsets": touch_ends(jax.random.randint(key_list[1], (N_STRIP, N_ALONG, 2), 0, min(ROWS, COLS) // 2), jax.random.fold_in(key_list[1], 1), 0, (min(ROWS, COLS) // 2) - 1).astype(jnp.int32),
    }


box_radius = 4


def box_sum(field):
    height, width = field.shape
    padded = jnp.pad(field, ((box_radius, box_radius), (0, 0)))
    rows_total = padded[0:height]
    for shift_k in range(1, 2 * box_radius + 1):
        rows_total = rows_total + padded[shift_k:shift_k + height]
    padded = jnp.pad(rows_total, ((0, 0), (box_radius, box_radius)))
    total = padded[:, 0:width]
    for shift_k in range(1, 2 * box_radius + 1):
        total = total + padded[:, shift_k:shift_k + width]
    return total


def pair_maps(guide, partner, roll_axis, base):
    counts = box_sum(jnp.ones_like(guide))
    mean_g = box_sum(guide) / counts
    var_g = box_sum(guide * guide) / counts - mean_g * mean_g
    filtered = []
    for level in range(DISP):
        shifted = jnp.roll(partner, -(base + level), axis=roll_axis)
        cost = jnp.abs(guide - shifted)
        mean_p = box_sum(cost) / counts
        cov = box_sum(guide * cost) / counts - mean_g * mean_p
        coef_a = cov / (var_g + 50.0)
        coef_b = mean_p - coef_a * mean_g
        filtered.append(box_sum(coef_a) / counts * guide + box_sum(coef_b) / counts)
    scores = -jnp.stack(filtered) * 4.0
    top = jnp.max(scores, axis=0)
    weights = jnp.exp(scores - top)
    prob = weights / jnp.sum(weights, axis=0)
    levels = jnp.arange(DISP).astype(jnp.float32)[:, None, None]
    disparity = jnp.sum(levels * prob, axis=0)
    confidence = jnp.sum(prob * prob, axis=0)
    return jnp.stack([disparity, confidence])


def reference(images, offsets):
    blocks = images.reshape(N_STRIP, ROWS, N_ALONG, COLS).transpose(0, 2, 1, 3)
    zeros_col = jnp.zeros((N_STRIP, 1, ROWS, COLS), jnp.float32)
    zeros_row = jnp.zeros((1, N_ALONG, ROWS, COLS), jnp.float32)
    forward = jnp.concatenate([blocks[:, 1:], zeros_col], axis=1)
    side = jnp.concatenate([blocks[1:], zeros_row], axis=0)
    count = N_STRIP * N_ALONG

    def one_block(items):
        guide, fwd_part, side_part, shift_pair = items
        return jnp.concatenate([pair_maps(guide, fwd_part, 1, shift_pair[0]), pair_maps(guide, side_part, 0, shift_pair[1])])

    maps = lax.map(one_block, (blocks.reshape(count, ROWS, COLS), forward.reshape(count, ROWS, COLS), side.reshape(count, ROWS, COLS), offsets.reshape(count, 2)))
    maps = maps.reshape(N_STRIP, N_ALONG, 4, ROWS, COLS)
    fwd_own = maps[:, :, 0:2]
    side_own = maps[:, :, 2:4]
    fwd_back = jnp.concatenate([jnp.zeros_like(fwd_own[:, 0:1]), fwd_own[:, :-1]], axis=1)
    side_back = jnp.concatenate([jnp.zeros_like(side_own[0:1]), side_own[:-1]], axis=0)
    full = jnp.concatenate([fwd_own, fwd_back, side_own, side_back], axis=2)
    return full.transpose(2, 0, 3, 1, 4).reshape(8, N_STRIP * ROWS, N_ALONG * COLS)
```

```python
import functools
import math

import jax
import jax.numpy as jnp
from jax import lax
from jax.experimental import pallas as pl
from jax.experimental.pallas import tpu as pltpu
from jax.sharding import PartitionSpec as P

DISP = 16
RADIUS = 4
LANES, SUBS = 128, 8
GROUP = 4
CENTRE = 128.0
VMEM_LIMIT = 24 * 2**20
f32, bf16, i32 = jnp.float32, jnp.bfloat16, jnp.int32
IN_VMEM = pl.BlockSpec(memory_space=pltpu.VMEM)
IN_SMEM = pl.BlockSpec(memory_space=pltpu.SMEM)
IN_ANY = pl.BlockSpec(memory_space=pl.ANY)


def iota(axis):
    return lax.broadcasted_iota(i32, (SUBS, LANES), axis)


def loop(n, body, unroll=True):
    lax.fori_loop(0, n, lambda i, c: (body(i), c)[1], 0, unroll=unroll)


def swap(x, n):
    return jnp.take_along_axis(x, iota(1) ^ n, axis=1, mode="promise_in_bounds")


def sums(x):
    front = [x[0]]
    for i in range(1, 8):
        front.append(front[-1] + x[i])
    back = [front[7]] + [x[7]] * 7
    for i in range(6, 0, -1):
        back[i] = back[i + 1] + x[i]
    return front, back


def box_cols(x):
    lane = iota(1)
    fa, ba = sums(x[:8])
    fb, bb = sums(x[8:])
    before = lambda y: jnp.where(lane >= GROUP, pltpu.roll(y, GROUP, 1), 0.0)
    after = lambda y: jnp.where(lane < LANES - GROUP, pltpu.roll(y, LANES - GROUP, 1), 0.0)
    out = [before(bb[k + 4]) + fa[k + 4] for k in range(4)]
    out += [ba[k] + fb[k] for k in range(8)]
    return out + [bb[k] + after(fa[k]) for k in range(4)]


def box_rows(x):
    sub = iota(0)
    front, back = sums(x)
    before = lambda y: jnp.where(sub >= 1, pltpu.roll(y, 1, 0), 0.0)
    after = lambda y: jnp.where(sub < SUBS - 1, pltpu.roll(y, SUBS - 1, 0), 0.0)
    return [before(back[j + 4]) + front[j + 4] for j in range(4)] + [back[j] + after(front[j]) for j in range(4)]


def make_order(order_ref):
    width = order_ref.shape[0]
    nv = width // LANES
    row = lax.broadcasted_iota(i32, (width, LANES), 0)
    lane = lax.broadcasted_iota(i32, (width, LANES), 1)
    for v in range(nv):
        order_ref[:, v * LANES:(v + 1) * LANES] = jnp.where(row == nv * lane + v, 1.0, 0.0).astype(bf16)


def reorder(x, order_ref, back=False):
    rows = x.shape[0]
    hi = x.astype(bf16)
    rest = x - hi.astype(f32)
    mid = rest.astype(bf16)
    low = (rest - mid.astype(f32)).astype(bf16)
    dims = (((1,), (1 if back else 0,)), ((), ()))
    y = lax.dot_general(jnp.concatenate([hi, mid, low]), order_ref[...], dims, preferred_element_type=f32)
    return (y[:rows] + y[rows:2 * rows]) + y[2 * rows:]


def put(ref, x):
    for v in range(ref.shape[0]):
        ref[v] = x[:, v * LANES:(v + 1) * LANES]


def inverse_counts(inv_ref, height, width):
    lane, sub = iota(1), iota(0)
    kk = inv_ref.shape[1]
    count = lambda i, n: 1.0 / (jnp.minimum(i + RADIUS, n - 1) - jnp.maximum(i - RADIUS, 0) + 1).astype(f32)
    cols = [count(lane // GROUP * kk + k, width) for k in range(kk)]
    for j in range(8):
        row = count(sub * 8 + j, height)
        for k in range(kk):
            inv_ref[j, k] = row * cols[k]


def guide_stats(v_ref, stats, inv_ref, p_ref, q_ref):
    g_ref, a1_ref, a2_ref, mean_ref = stats
    nv, kk = v_ref.shape[0], inv_ref.shape[1]
    first_lane = iota(1) // GROUP * GROUP

    def spread(h):
        for j in range(8):
            for v in range(nv):
                x = v_ref[v, pl.ds(j, SUBS, stride=8)]
                g_ref[j, nv * h + v] = jnp.take_along_axis(x, first_lane + h, axis=1, mode="promise_in_bounds")
    loop(GROUP, spread, 1)

    def first(j):
        g = [g_ref[j, k] for k in range(kk)]
        for k, y in enumerate(box_cols(g)):
            p_ref[j, k] = y
        for k, y in enumerate(box_cols([x * x for x in g])):
            q_ref[j, k] = y
    loop(8, first)

    def second(k):
        s1 = box_rows([p_ref[j, k] for j in range(8)])
        s2 = box_rows([q_ref[j, k] for j in range(8)])
        for j in range(8):
            inv = inv_ref[j, k]
            mean = s1[j] * inv
            a1 = inv / (s2[j] * inv - mean * mean + 50.0)
            a1_ref[j, k] = a1
            a2_ref[j, k] = a1 * mean
            mean_ref[j, k] = mean
    loop(kk, second)


def forward_partner(v_ref, y_ref, t):
    nv = v_ref.shape[0]

    def body(m):
        n = m + t
        a = lax.rem(LANES - lax.rem(lax.div(n, nv), LANES), LANES)
        for j in range(8):
            y_ref[m, j] = pltpu.roll(v_ref[lax.rem(n, nv), pl.ds(j, SUBS, stride=8)], a, 1)
    loop(y_ref.shape[0], body)


def side_partner(v2_ref, z_ref, t):
    nv, height = v2_ref.shape[0], v2_ref.shape[1] // 2
    odd, upper = iota(1) % 2 == 1, iota(1) % GROUP >= 2

    def one(m):
        start = [lax.rem(m + t + GROUP * h, height) for h in range(GROUP)]
        for v in range(nv):
            x = [v2_ref[v, pl.ds(start[h], SUBS, stride=8)] for h in range(GROUP)]
            for n in (0, 2):
                z_ref[m, nv * n + v] = jnp.where(odd, swap(x[n + 1], 1), x[n])
                z_ref[m, nv * (n + 1) + v] = jnp.where(odd, x[n + 1], swap(x[n], 1))
    loop(z_ref.shape[0], one)

    def two(m):
        for v in range(nv):
            for n in (0, 1):
                x, y = z_ref[m, nv * n + v], z_ref[m, nv * (n + 2) + v]
                z_ref[m, nv * n + v] = jnp.where(upper, swap(y, 2), x)
                z_ref[m, nv * (n + 2) + v] = jnp.where(upper, y, swap(x, 2))
    loop(z_ref.shape[0], two)


def pair_maps(partner, stats, inv_ref, work, out_ref):
    g_ref, a1_ref, a2_ref, mean_ref = stats
    p_ref, q_ref, a_ref, b_ref, score_ref = work
    kk = g_ref.shape[1]
    levels = DISP // GROUP

    def level(d):
        def first(j):
            g = [g_ref[j, k] for k in range(kk)]
            cost = [jnp.abs(g[k] - partner(j, k, d)) for k in range(kk)]
            for k, y in enumerate(box_cols(cost)):
                p_ref[j, k] = y
            for k, y in enumerate(box_cols([x * y for x, y in zip(g, cost)])):
                q_ref[j, k] = y
        loop(8, first)

        def second(k):
            p = box_rows([p_ref[j, k] for j in range(8)])
            q = box_rows([q_ref[j, k] for j in range(8)])
            ca = [q[j] * a1_ref[j, k] - p[j] * a2_ref[j, k] for j in range(8)]
            cb = [p[j] * inv_ref[j, k] - ca[j] * mean_ref[j, k] for j in range(8)]
            for j, y in enumerate(box_rows(ca)):
                a_ref[j, k] = y
            for j, y in enumerate(box_rows(cb)):
                b_ref[j, k] = y
        loop(kk, second)

        def third(j):
            a = box_cols([a_ref[j, k] for k in range(kk)])
            b = box_cols([b_ref[j, k] for k in range(kk)])
            for k in range(kk):
                score_ref[d, j, k] = (a[k] * g_ref[j, k] + b[k]) * (inv_ref[j, k] * (-4.0 * math.log2(math.e)))
        loop(8, third)
    loop(levels, level, 1)

    nv = kk // GROUP
    odd, upper = iota(1) % 2 == 1, iota(1) % GROUP >= 2
    lane_level = (iota(1) % GROUP * levels).astype(f32)

    def tops(j):
        for k in range(kk):
            top = functools.reduce(jnp.maximum, [score_ref[d, j, k] for d in range(levels)])
            top = jnp.maximum(top, swap(top, 1))
            b_ref[j, k] = jnp.maximum(top, swap(top, 2))
    loop(8, tops)

    def weights(j):
        for k in range(kk):
            w = [jnp.exp2(score_ref[d, j, k] - b_ref[j, k]) for d in range(levels)]
            s = w[-1]
            t = s
            for d in range(levels - 2, 0, -1):
                s = s + w[d]
                t = t + s
            s = s + w[0]
            p_ref[j, k] = s
            q_ref[j, k] = t + lane_level * s
            a_ref[j, k] = functools.reduce(jnp.add, [x * x for x in w])
    loop(8, weights, 1)

    def halves(j):
        for v in range(nv):
            for ref in (p_ref, q_ref, a_ref):
                x = [ref[j, nv * h + v] for h in range(GROUP)]
                for n in (0, 2):
                    ref[j, n // 2 * nv + v] = jnp.where(odd, x[n + 1], x[n]) + swap(jnp.where(odd, x[n], x[n + 1]), 1)
    loop(8, halves)

    height = out_ref.shape[1] // 2

    def last(j):
        for v in range(nv):
            lo, hi = ([ref[j, n * nv + v] for ref in (p_ref, q_ref, a_ref)] for n in range(2))
            s, t, u = (jnp.where(upper, y, x) + swap(jnp.where(upper, x, y), 2) for x, y in zip(lo, hi))
            r = 1.0 / s
            out_ref[v, pl.ds(j, SUBS, stride=8)] = t * r
            out_ref[v, pl.ds(height + j, SUBS, stride=8)] = u * (r * r)
    loop(8, last)


def restore(out_ref, order_ref):
    return reorder(jnp.concatenate([out_ref[v] for v in range(out_ref.shape[0])], axis=1), order_ref, back=True)


def field(kk, *lead):
    return (*lead, 8, kk, SUBS, LANES)


def call(body, ins, in_specs, outs, out_specs, scratch, flops, name):
    return pl.pallas_call(
        body, in_specs=in_specs, out_specs=out_specs, out_shape=outs, scratch_shapes=scratch, name=name,
        compiler_params=pltpu.CompilerParams(vmem_limit_bytes=VMEM_LIMIT),
        cost_estimate=pl.CostEstimate(flops=flops, bytes_accessed=2**20, transcendentals=0),
    )(*ins)


def per_device(images, offsets):
    height, width = images.shape
    kk = width // LANES * GROUP
    nv = width // LANES
    assert height == 8 * SUBS and kk == DISP
    tile_field = jax.ShapeDtypeStruct(field(kk), f32)
    vmem = lambda *shape: pltpu.VMEM(shape, f32)
    work = [vmem(*field(kk))] * 4 + [vmem(*field(kk, DISP // GROUP))]
    base = offsets[0, 0]
    strip = lax.axis_index("strip")

    def shifted(value, axis, steps):
        n = lax.axis_size(axis)
        return lax.ppermute(value, axis, [(i, i + steps) for i in range(max(0, -steps), min(n, n - steps))])

    def pack(base_ref, image_ref, out_ref):
        out_ref[:height] = image_ref[...]
        out_ref[height:] = jnp.full((SUBS, width), base_ref[1].astype(f32))

    def prepare(image_ref, order_ref, v_ref, inv_ref, g_ref, a1_ref, a2_ref, mean_ref, p_ref, q_ref):
        make_order(order_ref)
        inverse_counts(inv_ref, height, width)
        put(v_ref, reorder(image_ref[...] - CENTRE, order_ref))
        guide_stats(v_ref, (g_ref, a1_ref, a2_ref, mean_ref), inv_ref, p_ref, q_ref)

    def forward(base_ref, other_ref, order_ref, inv_ref, g_ref, a1_ref, a2_ref, mean_ref, out_ref, *scratch):
        *work_refs, v_ref, y_ref, maps_ref = scratch
        put(v_ref, reorder(other_ref[...] - CENTRE, order_ref))
        forward_partner(v_ref, y_ref, base_ref[0])
        pair_maps(lambda j, k, d: y_ref[k + d, j], (g_ref, a1_ref, a2_ref, mean_ref), inv_ref, work_refs, maps_ref)
        maps = restore(maps_ref, order_ref)
        out_ref[0] = maps[:height]
        out_ref[1] = maps[height:]

    def side(base_ref, own_ref, back_ref, other_ref, order_ref, inv_ref, g_ref, a1_ref, a2_ref, mean_ref, first_ref, out_ref, *scratch):
        *work_refs, v2_ref, z_ref, maps_ref, res_ref, b0, b1, b2, b3, sems = scratch
        copies = [pltpu.make_async_copy(first_ref, out_ref.at[0:2], sems.at[0])]
        copies[0].start()
        partner = lambda j, k, d: z_ref[j + d, k]

        def send(n, row):
            copies.append(pltpu.make_async_copy(res_ref.at[n], out_ref.at[row:row + 2], sems.at[n + 1]))
            copies[-1].start()

        def finish(n):
            maps = restore(maps_ref, order_ref)
            res_ref[n, 0] = maps[:height]
            res_ref[n, 1] = maps[height:]

        def twice(x):
            put(v2_ref, jnp.concatenate([x, x]))

        twice(reorder(other_ref[...] - CENTRE, order_ref))
        side_partner(v2_ref, z_ref, base_ref[1])
        pair_maps(partner, (g_ref, a1_ref, a2_ref, mean_ref), inv_ref, work_refs, maps_ref)
        finish(0)
        send(0, 4)

        @pl.when(base_ref[2] > 0)
        def _():
            twice(reorder(back_ref[:height] - CENTRE, order_ref))
            guide_stats(v2_ref.at[:, :height], (b0, b1, b2, b3), inv_ref, work_refs[0], work_refs[1])
            for v in range(nv):
                v2_ref[v, :height] = own_ref[v]
                v2_ref[v, height:] = own_ref[v]
            t = jnp.max(back_ref[height:, :LANES]).astype(i32)
            side_partner(v2_ref, z_ref, t)
            pair_maps(partner, (b0, b1, b2, b3), inv_ref, work_refs, maps_ref)
            finish(1)

        @pl.when(base_ref[2] == 0)
        def _():
            res_ref[1] = jnp.zeros(res_ref.shape[1:], f32)

        send(1, 6)
        for copy in copies:
            copy.wait()

    fwd_image = shifted(images, "along", -1)
    side_image = shifted(images, "strip", -1)
    scalars = jnp.concatenate([base, strip.astype(i32)[None]])
    packed = call(
        pack, (scalars, images), [IN_SMEM, IN_VMEM],
        jax.ShapeDtypeStruct((height + SUBS, width), f32), IN_VMEM, [], 2**16, "pack",
    )
    back_image = shifted(packed, "strip", 1)
    order, own, inv, *stats = call(
        prepare, (images,), [IN_VMEM],
        [jax.ShapeDtypeStruct((width, width), bf16), jax.ShapeDtypeStruct((nv, height, LANES), f32)] + [tile_field] * 5,
        [IN_VMEM] * 7, [vmem(*field(kk))] * 2, 2**26, "prepare",
    )
    fwd_image, side_image, back_image = lax.optimization_barrier((fwd_image, side_image, back_image))
    maps_shape = vmem(nv, 2 * height, LANES)
    fwd_maps = call(
        forward, (scalars, fwd_image, order, inv, *stats), [IN_SMEM] + [IN_VMEM] * 7,
        jax.ShapeDtypeStruct((2, height, width), f32), IN_VMEM,
        work + [vmem(nv, height, LANES), vmem(kk + 3, 8, SUBS, LANES), maps_shape], 2**28, "forward",
    )
    fwd_back = shifted(fwd_maps, "along", 1)
    out = call(
        side, (scalars, own, back_image, side_image, order, inv, *stats, fwd_maps), [IN_SMEM] + [IN_VMEM] * 10,
        jax.ShapeDtypeStruct((8, height, width), f32), IN_ANY,
        work + [maps_shape, vmem(8 + 3, kk, SUBS, LANES), maps_shape, vmem(2, 2, height, width)]
        + [vmem(*field(kk))] * 4 + [pltpu.SemaphoreType.DMA((3,))], 2**29, "side",
    )
    return lax.dynamic_update_slice(out, fwd_back, (2, 0, 0))


def solution(mesh):
    return jax.shard_map(
        per_device, mesh=mesh, in_specs=(P("strip", "along"), P("strip", "along", None)),
        out_specs=P(None, "strip", "along"), check_vma=False,
    )
```

```python
import functools
import math

import jax
import jax.numpy as jnp
from jax import lax
from jax.experimental import pallas as pl
from jax.experimental.pallas import tpu as pltpu
from jax.sharding import PartitionSpec as P

DISP = 16
RADIUS = 4
LANES, SUBS = 128, 8
GROUP = 4
CENTRE = 128.0
VMEM_LIMIT = 24 * 2**20
f32, bf16, i32 = jnp.float32, jnp.bfloat16, jnp.int32
IN_VMEM = pl.BlockSpec(memory_space=pltpu.VMEM)
IN_SMEM = pl.BlockSpec(memory_space=pltpu.SMEM)
IN_ANY = pl.BlockSpec(memory_space=pl.ANY)


def iota(axis):
    return lax.broadcasted_iota(i32, (SUBS, LANES), axis)


def loop(n, body, unroll=True):
    lax.fori_loop(0, n, lambda i, c: (body(i), c)[1], 0, unroll=unroll)


def swap(x, n):
    return jnp.take_along_axis(x, iota(1) ^ n, axis=1, mode="promise_in_bounds")


def sums(x):
    front = [x[0]]
    for i in range(1, 8):
        front.append(front[-1] + x[i])
    back = [front[7]] + [x[7]] * 7
    for i in range(6, 0, -1):
        back[i] = back[i + 1] + x[i]
    return front, back


def box_cols(x):
    lane = iota(1)
    fa, ba = sums(x[:8])
    fb, bb = sums(x[8:])
    before = lambda y: jnp.where(lane >= GROUP, pltpu.roll(y, GROUP, 1), 0.0)
    after = lambda y: jnp.where(lane < LANES - GROUP, pltpu.roll(y, LANES - GROUP, 1), 0.0)
    out = [before(bb[k + 4]) + fa[k + 4] for k in range(4)]
    out += [ba[k] + fb[k] for k in range(8)]
    return out + [bb[k] + after(fa[k]) for k in range(4)]


def box_rows(x):
    sub = iota(0)
    front, back = sums(x)
    before = lambda y: jnp.where(sub >= 1, pltpu.roll(y, 1, 0), 0.0)
    after = lambda y: jnp.where(sub < SUBS - 1, pltpu.roll(y, SUBS - 1, 0), 0.0)
    return [before(back[j + 4]) + front[j + 4] for j in range(4)] + [back[j] + after(front[j]) for j in range(4)]


def make_order(order_ref):
    width = order_ref.shape[0]
    nv = width // LANES
    row = lax.broadcasted_iota(i32, (width, LANES), 0)
    lane = lax.broadcasted_iota(i32, (width, LANES), 1)
    for v in range(nv):
        order_ref[:, v * LANES:(v + 1) * LANES] = jnp.where(row == nv * lane + v, 1.0, 0.0).astype(bf16)


def reorder(x, order_ref, back=False):
    rows = x.shape[0]
    hi = x.astype(bf16)
    rest = x - hi.astype(f32)
    mid = rest.astype(bf16)
    low = (rest - mid.astype(f32)).astype(bf16)
    dims = (((1,), (1 if back else 0,)), ((), ()))
    y = lax.dot_general(jnp.concatenate([hi, mid, low]), order_ref[...], dims, preferred_element_type=f32)
    return (y[:rows] + y[rows:2 * rows]) + y[2 * rows:]


def put(ref, x):
    for v in range(ref.shape[0]):
        ref[v] = x[:, v * LANES:(v + 1) * LANES]


def inverse_counts(inv_ref, height, width):
    lane, sub = iota(1), iota(0)
    kk = inv_ref.shape[1]
    count = lambda i, n: 1.0 / (jnp.minimum(i + RADIUS, n - 1) - jnp.maximum(i - RADIUS, 0) + 1).astype(f32)
    cols = [count(lane // GROUP * kk + k, width) for k in range(kk)]
    for j in range(8):
        row = count(sub * 8 + j, height)
        for k in range(kk):
            inv_ref[j, k] = row * cols[k]


def guide_stats(v_ref, stats, inv_ref, p_ref, q_ref):
    g_ref, a1_ref, a2_ref, mean_ref = stats
    nv, kk = v_ref.shape[0], inv_ref.shape[1]
    first_lane = iota(1) // GROUP * GROUP

    def spread(h):
        for j in range(8):
            for v in range(nv):
                x = v_ref[v, pl.ds(j, SUBS, stride=8)]
                g_ref[j, nv * h + v] = jnp.take_along_axis(x, first_lane + h, axis=1, mode="promise_in_bounds")
    loop(GROUP, spread, 1)

    def first(j):
        g = [g_ref[j, k] for k in range(kk)]
        for k, y in enumerate(box_cols(g)):
            p_ref[j, k] = y
        for k, y in enumerate(box_cols([x * x for x in g])):
            q_ref[j, k] = y
    loop(8, first)

    def second(k):
        s1 = box_rows([p_ref[j, k] for j in range(8)])
        s2 = box_rows([q_ref[j, k] for j in range(8)])
        for j in range(8):
            inv = inv_ref[j, k]
            mean = s1[j] * inv
            a1 = inv / (s2[j] * inv - mean * mean + 50.0)
            a1_ref[j, k] = a1
            a2_ref[j, k] = a1 * mean
            mean_ref[j, k] = mean
    loop(kk, second)


def forward_partner(v_ref, y_ref, t):
    nv = v_ref.shape[0]

    def body(m):
        n = m + t
        a = lax.rem(LANES - lax.rem(lax.div(n, nv), LANES), LANES)
        for j in range(8):
            y_ref[m, j] = pltpu.roll(v_ref[lax.rem(n, nv), pl.ds(j, SUBS, stride=8)], a, 1)
    loop(y_ref.shape[0], body)


def side_partner(v2_ref, z_ref, t):
    nv, height = v2_ref.shape[0], v2_ref.shape[1] // 2
    odd, upper = iota(1) % 2 == 1, iota(1) % GROUP >= 2

    def one(m):
        start = [lax.rem(m + t + GROUP * h, height) for h in range(GROUP)]
        for v in range(nv):
            x = [v2_ref[v, pl.ds(start[h], SUBS, stride=8)] for h in range(GROUP)]
            for n in (0, 2):
                z_ref[m, nv * n + v] = jnp.where(odd, swap(x[n + 1], 1), x[n])
                z_ref[m, nv * (n + 1) + v] = jnp.where(odd, x[n + 1], swap(x[n], 1))
    loop(z_ref.shape[0], one)

    def two(m):
        for v in range(nv):
            for n in (0, 1):
                x, y = z_ref[m, nv * n + v], z_ref[m, nv * (n + 2) + v]
                z_ref[m, nv * n + v] = jnp.where(upper, swap(y, 2), x)
                z_ref[m, nv * (n + 2) + v] = jnp.where(upper, y, swap(x, 2))
    loop(z_ref.shape[0], two)


def pair_maps(partner, stats, inv_ref, work, out_ref):
    g_ref, a1_ref, a2_ref, mean_ref = stats
    p_ref, q_ref, a_ref, b_ref, score_ref = work
    kk = g_ref.shape[1]
    levels = DISP // GROUP

    def level(d):
        def first(j):
            g = [g_ref[j, k] for k in range(kk)]
            cost = [jnp.abs(g[k] - partner(j, k, d)) for k in range(kk)]
            for k, y in enumerate(box_cols(cost)):
                p_ref[j, k] = y
            for k, y in enumerate(box_cols([x * y for x, y in zip(g, cost)])):
                q_ref[j, k] = y
        loop(8, first)

        def second(k):
            p = box_rows([p_ref[j, k] for j in range(8)])
            q = box_rows([q_ref[j, k] for j in range(8)])
            ca = [q[j] * a1_ref[j, k] - p[j] * a2_ref[j, k] for j in range(8)]
            cb = [p[j] * inv_ref[j, k] - ca[j] * mean_ref[j, k] for j in range(8)]
            for j, y in enumerate(box_rows(ca)):
                a_ref[j, k] = y
            for j, y in enumerate(box_rows(cb)):
                b_ref[j, k] = y
        loop(kk, second)

        def third(j):
            a = box_cols([a_ref[j, k] for k in range(kk)])
            b = box_cols([b_ref[j, k] for k in range(kk)])
            for k in range(kk):
                score_ref[d, j, k] = (a[k] * g_ref[j, k] + b[k]) * (inv_ref[j, k] * (-4.0 * math.log2(math.e)))
        loop(8, third)
    loop(levels, level, 1)

    nv = kk // GROUP
    odd, upper = iota(1) % 2 == 1, iota(1) % GROUP >= 2
    lane_level = (iota(1) % GROUP * levels).astype(f32)

    def tops(j):
        for k in range(kk):
            top = functools.reduce(jnp.maximum, [score_ref[d, j, k] for d in range(levels)])
            top = jnp.maximum(top, swap(top, 1))
            b_ref[j, k] = jnp.maximum(top, swap(top, 2))
    loop(8, tops)

    def weights(j):
        for k in range(kk):
            w = [jnp.exp2(score_ref[d, j, k] - b_ref[j, k]) for d in range(levels)]
            s = w[-1]
            t = s
            for d in range(levels - 2, 0, -1):
                s = s + w[d]
                t = t + s
            s = s + w[0]
            p_ref[j, k] = s
            q_ref[j, k] = t + lane_level * s
            a_ref[j, k] = functools.reduce(jnp.add, [x * x for x in w])
    loop(8, weights, 1)

    def halves(j):
        for v in range(nv):
            for ref in (p_ref, q_ref, a_ref):
                x = [ref[j, nv * h + v] for h in range(GROUP)]
                for n in (0, 2):
                    ref[j, n // 2 * nv + v] = jnp.where(odd, x[n + 1], x[n]) + swap(jnp.where(odd, x[n], x[n + 1]), 1)
    loop(8, halves)

    height = out_ref.shape[1] // 2

    def last(j):
        for v in range(nv):
            lo, hi = ([ref[j, n * nv + v] for ref in (p_ref, q_ref, a_ref)] for n in range(2))
            s, t, u = (jnp.where(upper, y, x) + swap(jnp.where(upper, x, y), 2) for x, y in zip(lo, hi))
            r = 1.0 / s
            out_ref[v, pl.ds(j, SUBS, stride=8)] = t * r
            out_ref[v, pl.ds(height + j, SUBS, stride=8)] = u * (r * r)
    loop(8, last)


def restore(out_ref, order_ref):
    return reorder(jnp.concatenate([out_ref[v] for v in range(out_ref.shape[0])], axis=1), order_ref, back=True)


def field(kk, *lead):
    return (*lead, 8, kk, SUBS, LANES)


def call(body, ins, in_specs, outs, out_specs, scratch, flops, name, aliases={}):
    return pl.pallas_call(
        body, in_specs=in_specs, out_specs=out_specs, out_shape=outs, scratch_shapes=scratch, name=name,
        input_output_aliases=aliases,
        compiler_params=pltpu.CompilerParams(vmem_limit_bytes=VMEM_LIMIT),
        cost_estimate=pl.CostEstimate(flops=flops, bytes_accessed=2**20, transcendentals=0),
    )(*ins)


def per_device(images, offsets):
    height, width = images.shape
    kk = width // LANES * GROUP
    nv = width // LANES
    assert height == 8 * SUBS and kk == DISP
    tile_field = jax.ShapeDtypeStruct(field(kk), f32)
    vmem = lambda *shape: pltpu.VMEM(shape, f32)
    work = [vmem(*field(kk))] * 4 + [vmem(*field(kk, DISP // GROUP))]

    def shifted(value, axis, steps):
        n = lax.axis_size(axis)
        return lax.ppermute(value, axis, [(i, i + steps) for i in range(max(0, -steps), min(n, n - steps))])

    def prepare(base_ref, image_ref, order_ref, v_ref, packed_ref, inv_ref, g_ref, a1_ref, a2_ref, mean_ref, p_ref, q_ref):
        packed_ref[:height] = image_ref[...]
        packed_ref[height:] = jnp.full((SUBS, width), base_ref[0, 0, 0].astype(f32))
        make_order(order_ref)
        inverse_counts(inv_ref, height, width)
        put(v_ref, reorder(image_ref[...] - CENTRE, order_ref))
        guide_stats(v_ref, (g_ref, a1_ref, a2_ref, mean_ref), inv_ref, p_ref, q_ref)

    def side(base_ref, other_ref, order_ref, inv_ref, g_ref, a1_ref, a2_ref, mean_ref, out_ref, *scratch):
        *work_refs, v2_ref, z_ref, maps_ref = scratch
        x = reorder(other_ref[...] - CENTRE, order_ref)
        put(v2_ref, jnp.concatenate([x, x]))
        side_partner(v2_ref, z_ref, base_ref[0, 0, 1])
        pair_maps(lambda j, k, d: z_ref[j + d, k], (g_ref, a1_ref, a2_ref, mean_ref), inv_ref, work_refs, maps_ref)
        maps = restore(maps_ref, order_ref)
        out_ref[0] = maps[:height]
        out_ref[1] = maps[height:]

    def finish(maps_ref, order_ref, res_ref, out_ref, sem):
        maps = restore(maps_ref, order_ref)
        res_ref[0] = maps[:height]
        res_ref[1] = maps[height:]
        copy = pltpu.make_async_copy(res_ref, out_ref, sem)
        copy.start()
        return copy

    def forward(base_ref, other_ref, order_ref, inv_ref, g_ref, a1_ref, a2_ref, mean_ref, side_ref, out_ref, *scratch):
        *work_refs, v_ref, y_ref, maps_ref, res_ref, sems = scratch
        copy = pltpu.make_async_copy(side_ref, out_ref.at[4:6], sems.at[0])
        copy.start()
        put(v_ref, reorder(other_ref[...] - CENTRE, order_ref))
        forward_partner(v_ref, y_ref, base_ref[0, 0, 0])
        pair_maps(lambda j, k, d: y_ref[k + d, j], (g_ref, a1_ref, a2_ref, mean_ref), inv_ref, work_refs, maps_ref)
        finish(maps_ref, order_ref, res_ref, out_ref.at[0:2], sems.at[1]).wait()
        copy.wait()

    def backward(own_ref, back_ref, order_ref, inv_ref, side_ref, old_ref, out_ref, *scratch):
        *work_refs, v_ref, y_ref, maps_ref, res_ref, b0, b1, b2, b3, sems = scratch
        along = lax.axis_index("along")
        received = pltpu.make_async_copy(side_ref, out_ref.at[6:8], sems.at[1])
        received.start()

        @pl.when(along > 0)
        def _():
            put(v_ref, reorder(back_ref[:height] - CENTRE, order_ref))
            guide_stats(v_ref, (b0, b1, b2, b3), inv_ref, work_refs[0], work_refs[1])
            forward_partner(own_ref, y_ref, jnp.max(back_ref[height:, :LANES]).astype(i32))
            pair_maps(lambda j, k, d: y_ref[k + d, j], (b0, b1, b2, b3), inv_ref, work_refs, maps_ref)
            finish(maps_ref, order_ref, res_ref, out_ref.at[2:4], sems.at[0]).wait()

        @pl.when(along == 0)
        def _():
            res_ref[...] = jnp.zeros_like(res_ref)
            copy = pltpu.make_async_copy(res_ref, out_ref.at[2:4], sems.at[0])
            copy.start()
            copy.wait()
        received.wait()

    maps_shape = vmem(nv, 2 * height, LANES)
    fwd_image = shifted(images, "along", -1)
    side_image = shifted(images, "strip", -1)
    order, own, packed, inv, *stats = call(
        prepare, (offsets, images), [IN_SMEM, IN_VMEM],
        [jax.ShapeDtypeStruct((width, width), bf16), jax.ShapeDtypeStruct((nv, height, LANES), f32),
         jax.ShapeDtypeStruct((height + SUBS, width), f32)] + [tile_field] * 5,
        [IN_VMEM] * 8, [vmem(*field(kk))] * 2, 2**26, "prepare",
    )
    back_image = shifted(packed, "along", 1)
    fwd_image, side_image = lax.optimization_barrier((fwd_image, side_image))
    side_maps = call(
        side, (offsets, side_image, order, inv, *stats), [IN_SMEM] + [IN_VMEM] * 7,
        jax.ShapeDtypeStruct((2, height, width), f32), IN_VMEM,
        work + [maps_shape, vmem(8 + 3, kk, SUBS, LANES), maps_shape], 2**28, "side",
    )
    side_back = shifted(side_maps, "strip", 1)
    pair_scratch = work + [vmem(nv, height, LANES), vmem(kk + 3, 8, SUBS, LANES), maps_shape, vmem(2, height, width)]
    whole = jax.ShapeDtypeStruct((8, height, width), f32)
    out = call(
        forward, (offsets, fwd_image, order, inv, *stats, side_maps), [IN_SMEM] + [IN_VMEM] * 8,
        whole, IN_ANY, pair_scratch + [pltpu.SemaphoreType.DMA((2,))], 2**28, "forward",
    )
    return call(
        backward, (own, back_image, order, inv, side_back, out), [IN_VMEM] * 5 + [IN_ANY],
        whole, IN_ANY, pair_scratch + [vmem(*field(kk))] * 4 + [pltpu.SemaphoreType.DMA((2,))], 2**28, "backward", {5: 0},
    )


def solution(mesh):
    return jax.shard_map(
        per_device, mesh=mesh, in_specs=(P("strip", "along"), P("strip", "along", None)),
        out_specs=P(None, "strip", "along"), check_vma=False,
    )
```

```python
import functools
import math

import jax
import jax.numpy as jnp
from jax import lax
from jax.experimental import pallas as pl
from jax.experimental.pallas import tpu as pltpu
from jax.sharding import PartitionSpec as P

DISP = 16
RADIUS = 4
LANES, SUBS = 128, 8
GROUP = 4
CENTRE = 128.0
VMEM_LIMIT = 24 * 2**20
f32, bf16, i32 = jnp.float32, jnp.bfloat16, jnp.int32
IN_VMEM = pl.BlockSpec(memory_space=pltpu.VMEM)
IN_SMEM = pl.BlockSpec(memory_space=pltpu.SMEM)
IN_ANY = pl.BlockSpec(memory_space=pl.ANY)


def iota(axis):
    return lax.broadcasted_iota(i32, (SUBS, LANES), axis)


def loop(n, body, unroll=True):
    lax.fori_loop(0, n, lambda i, c: (body(i), c)[1], 0, unroll=unroll)


def swap(x, n):
    return jnp.take_along_axis(x, iota(1) ^ n, axis=1, mode="promise_in_bounds")


def sums(x):
    front = [x[0]]
    for i in range(1, 8):
        front.append(front[-1] + x[i])
    back = [front[7]] + [x[7]] * 7
    for i in range(6, 0, -1):
        back[i] = back[i + 1] + x[i]
    return front, back


def box_cols(x):
    lane = iota(1)
    fa, ba = sums(x[:8])
    fb, bb = sums(x[8:])
    before = lambda y: jnp.where(lane >= GROUP, pltpu.roll(y, GROUP, 1), 0.0)
    after = lambda y: jnp.where(lane < LANES - GROUP, pltpu.roll(y, LANES - GROUP, 1), 0.0)
    out = [before(bb[k + 4]) + fa[k + 4] for k in range(4)]
    out += [ba[k] + fb[k] for k in range(8)]
    return out + [bb[k] + after(fa[k]) for k in range(4)]


def box_rows(x):
    sub = iota(0)
    front, back = sums(x)
    before = lambda y: jnp.where(sub >= 1, pltpu.roll(y, 1, 0), 0.0)
    after = lambda y: jnp.where(sub < SUBS - 1, pltpu.roll(y, SUBS - 1, 0), 0.0)
    return [before(back[j + 4]) + front[j + 4] for j in range(4)] + [back[j] + after(front[j]) for j in range(4)]


def make_order(order_ref):
    width = order_ref.shape[0]
    nv = width // LANES
    row = lax.broadcasted_iota(i32, (width, LANES), 0)
    lane = lax.broadcasted_iota(i32, (width, LANES), 1)
    for v in range(nv):
        order_ref[:, v * LANES:(v + 1) * LANES] = jnp.where(row == nv * lane + v, 1.0, 0.0).astype(bf16)


def reorder(x, order_ref, back=False):
    rows = x.shape[0]
    hi = x.astype(bf16)
    rest = x - hi.astype(f32)
    mid = rest.astype(bf16)
    low = (rest - mid.astype(f32)).astype(bf16)
    dims = (((1,), (1 if back else 0,)), ((), ()))
    y = lax.dot_general(jnp.concatenate([hi, mid, low]), order_ref[...], dims, preferred_element_type=f32)
    return (y[:rows] + y[rows:2 * rows]) + y[2 * rows:]


def put(ref, x):
    for v in range(ref.shape[0]):
        ref[v] = x[:, v * LANES:(v + 1) * LANES]


def inverse_counts(inv_ref, height, width):
    lane, sub = iota(1), iota(0)
    kk = inv_ref.shape[1]
    count = lambda i, n: 1.0 / (jnp.minimum(i + RADIUS, n - 1) - jnp.maximum(i - RADIUS, 0) + 1).astype(f32)
    cols = [count(lane // GROUP * kk + k, width) for k in range(kk)]
    for j in range(8):
        row = count(sub * 8 + j, height)
        for k in range(kk):
            inv_ref[j, k] = row * cols[k]


def guide_stats(v_ref, stats, inv_ref, p_ref, q_ref):
    g_ref, a1_ref, a2_ref, mean_ref = stats
    nv, kk = v_ref.shape[0], inv_ref.shape[1]
    first_lane = iota(1) // GROUP * GROUP

    def spread(h):
        for j in range(8):
            for v in range(nv):
                x = v_ref[v, pl.ds(j, SUBS, stride=8)]
                g_ref[j, nv * h + v] = jnp.take_along_axis(x, first_lane + h, axis=1, mode="promise_in_bounds")
    loop(GROUP, spread, 1)

    def first(j):
        g = [g_ref[j, k] for k in range(kk)]
        for k, y in enumerate(box_cols(g)):
            p_ref[j, k] = y
        for k, y in enumerate(box_cols([x * x for x in g])):
            q_ref[j, k] = y
    loop(8, first)

    def second(k):
        s1 = box_rows([p_ref[j, k] for j in range(8)])
        s2 = box_rows([q_ref[j, k] for j in range(8)])
        for j in range(8):
            inv = inv_ref[j, k]
            mean = s1[j] * inv
            a1 = inv / (s2[j] * inv - mean * mean + 50.0)
            a1_ref[j, k] = a1
            a2_ref[j, k] = a1 * mean
            mean_ref[j, k] = mean
    loop(kk, second)


def forward_partner(v_ref, y_ref, t):
    nv = v_ref.shape[0]

    def body(m):
        n = m + t
        a = lax.rem(LANES - lax.rem(lax.div(n, nv), LANES), LANES)
        for j in range(8):
            y_ref[m, j] = pltpu.roll(v_ref[lax.rem(n, nv), pl.ds(j, SUBS, stride=8)], a, 1)
    loop(y_ref.shape[0], body)


def side_partner(v2_ref, z_ref, t):
    nv, height = v2_ref.shape[0], v2_ref.shape[1] // 2
    odd, upper = iota(1) % 2 == 1, iota(1) % GROUP >= 2

    def one(m):
        start = [lax.rem(m + t + GROUP * h, height) for h in range(GROUP)]
        for v in range(nv):
            x = [v2_ref[v, pl.ds(start[h], SUBS, stride=8)] for h in range(GROUP)]
            for n in (0, 2):
                z_ref[m, nv * n + v] = jnp.where(odd, swap(x[n + 1], 1), x[n])
                z_ref[m, nv * (n + 1) + v] = jnp.where(odd, x[n + 1], swap(x[n], 1))
    loop(z_ref.shape[0], one)

    def two(m):
        for v in range(nv):
            for n in (0, 1):
                x, y = z_ref[m, nv * n + v], z_ref[m, nv * (n + 2) + v]
                z_ref[m, nv * n + v] = jnp.where(upper, swap(y, 2), x)
                z_ref[m, nv * (n + 2) + v] = jnp.where(upper, y, swap(x, 2))
    loop(z_ref.shape[0], two)


def pair_maps(partner, stats, inv_ref, work, out_ref):
    g_ref, a1_ref, a2_ref, mean_ref = stats
    p_ref, q_ref, a_ref, b_ref, score_ref = work
    kk = g_ref.shape[1]
    levels = DISP // GROUP

    def level(d):
        def first(j):
            g = [g_ref[j, k] for k in range(kk)]
            cost = [jnp.abs(g[k] - partner(j, k, d)) for k in range(kk)]
            for k, y in enumerate(box_cols(cost)):
                p_ref[j, k] = y
            for k, y in enumerate(box_cols([x * y for x, y in zip(g, cost)])):
                q_ref[j, k] = y
        loop(8, first)

        def second(k):
            p = box_rows([p_ref[j, k] for j in range(8)])
            q = box_rows([q_ref[j, k] for j in range(8)])
            ca = [q[j] * a1_ref[j, k] - p[j] * a2_ref[j, k] for j in range(8)]
            cb = [p[j] * inv_ref[j, k] - ca[j] * mean_ref[j, k] for j in range(8)]
            for j, y in enumerate(box_rows(ca)):
                a_ref[j, k] = y
            for j, y in enumerate(box_rows(cb)):
                b_ref[j, k] = y
        loop(kk, second)

        def third(j):
            a = box_cols([a_ref[j, k] for k in range(kk)])
            b = box_cols([b_ref[j, k] for k in range(kk)])
            for k in range(kk):
                score_ref[d, j, k] = (a[k] * g_ref[j, k] + b[k]) * (inv_ref[j, k] * (-4.0 * math.log2(math.e)))
        loop(8, third)
    loop(levels, level, 1)

    nv = kk // GROUP
    odd, upper = iota(1) % 2 == 1, iota(1) % GROUP >= 2
    lane_level = (iota(1) % GROUP * levels).astype(f32)

    def tops(j):
        for k in range(kk):
            top = functools.reduce(jnp.maximum, [score_ref[d, j, k] for d in range(levels)])
            top = jnp.maximum(top, swap(top, 1))
            b_ref[j, k] = jnp.maximum(top, swap(top, 2))
    loop(8, tops)

    def weights(j):
        for k in range(kk):
            w = [jnp.exp2(score_ref[d, j, k] - b_ref[j, k]) for d in range(levels)]
            s = w[-1]
            t = s
            for d in range(levels - 2, 0, -1):
                s = s + w[d]
                t = t + s
            s = s + w[0]
            p_ref[j, k] = s
            q_ref[j, k] = t + lane_level * s
            a_ref[j, k] = functools.reduce(jnp.add, [x * x for x in w])
    loop(8, weights, 1)

    def halves(j):
        for v in range(nv):
            for ref in (p_ref, q_ref, a_ref):
                x = [ref[j, nv * h + v] for h in range(GROUP)]
                for n in (0, 2):
                    ref[j, n // 2 * nv + v] = jnp.where(odd, x[n + 1], x[n]) + swap(jnp.where(odd, x[n], x[n + 1]), 1)
    loop(8, halves)

    height = out_ref.shape[1] // 2

    def last(j):
        for v in range(nv):
            lo, hi = ([ref[j, n * nv + v] for ref in (p_ref, q_ref, a_ref)] for n in range(2))
            s, t, u = (jnp.where(upper, y, x) + swap(jnp.where(upper, x, y), 2) for x, y in zip(lo, hi))
            r = 1.0 / s
            out_ref[v, pl.ds(j, SUBS, stride=8)] = t * r
            out_ref[v, pl.ds(height + j, SUBS, stride=8)] = u * (r * r)
    loop(8, last)


def restore(out_ref, order_ref):
    return reorder(jnp.concatenate([out_ref[v] for v in range(out_ref.shape[0])], axis=1), order_ref, back=True)


def field(kk, *lead):
    return (*lead, 8, kk, SUBS, LANES)


def call(body, ins, in_specs, outs, out_specs, scratch, flops, name, aliases={}):
    return pl.pallas_call(
        body, in_specs=in_specs, out_specs=out_specs, out_shape=outs, scratch_shapes=scratch, name=name,
        input_output_aliases=aliases,
        compiler_params=pltpu.CompilerParams(vmem_limit_bytes=VMEM_LIMIT),
        cost_estimate=pl.CostEstimate(flops=flops, bytes_accessed=2**20, transcendentals=0),
    )(*ins)


def per_device(images, offsets):
    height, width = images.shape
    kk = width // LANES * GROUP
    nv = width // LANES
    assert height == 8 * SUBS and kk == DISP
    tile_field = jax.ShapeDtypeStruct(field(kk), f32)
    vmem = lambda *shape: pltpu.VMEM(shape, f32)
    work = [vmem(*field(kk))] * 4 + [vmem(*field(kk, DISP // GROUP))]

    def shifted(value, axis, steps):
        n = lax.axis_size(axis)
        return lax.ppermute(value, axis, [(i, i + steps) for i in range(max(0, -steps), min(n, n - steps))])

    def prepare(base_ref, image_ref, order_ref, inv_ref, g_ref, a1_ref, a2_ref, mean_ref, v_ref, p_ref, q_ref):
        make_order(order_ref)
        inverse_counts(inv_ref, height, width)
        put(v_ref, reorder(image_ref[...] - CENTRE, order_ref))
        guide_stats(v_ref, (g_ref, a1_ref, a2_ref, mean_ref), inv_ref, p_ref, q_ref)

    def finish(maps_ref, order_ref, out_ref):
        maps = restore(maps_ref, order_ref)
        out_ref[0] = maps[:height]
        out_ref[1] = maps[height:]

    def side(base_ref, other_ref, order_ref, inv_ref, g_ref, a1_ref, a2_ref, mean_ref, out_ref, *scratch):
        *work_refs, v2_ref, z_ref, maps_ref = scratch
        x = reorder(other_ref[...] - CENTRE, order_ref)
        put(v2_ref, jnp.concatenate([x, x]))
        side_partner(v2_ref, z_ref, base_ref[0, 0, 1])
        pair_maps(lambda j, k, d: z_ref[j + d, k], (g_ref, a1_ref, a2_ref, mean_ref), inv_ref, work_refs, maps_ref)
        finish(maps_ref, order_ref, out_ref)

    def forward(base_ref, other_ref, order_ref, inv_ref, g_ref, a1_ref, a2_ref, mean_ref, out_ref, *scratch):
        *work_refs, v_ref, y_ref, maps_ref = scratch
        put(v_ref, reorder(other_ref[...] - CENTRE, order_ref))
        forward_partner(v_ref, y_ref, base_ref[0, 0, 0])
        pair_maps(lambda j, k, d: y_ref[k + d, j], (g_ref, a1_ref, a2_ref, mean_ref), inv_ref, work_refs, maps_ref)
        finish(maps_ref, order_ref, out_ref)

    def collect(rows, *refs):
        out_ref, sems = refs[-2:]
        copies = [pltpu.make_async_copy(refs[i], out_ref.at[row:row + 2], sems.at[i]) for i, row in enumerate(rows)]
        for copy in copies:
            copy.start()
        for copy in copies:
            copy.wait()

    maps_shape = vmem(nv, 2 * height, LANES)
    two_maps = jax.ShapeDtypeStruct((2, height, width), f32)
    whole = jax.ShapeDtypeStruct((8, height, width), f32)
    fwd_image = shifted(images, "along", -1)
    side_image = shifted(images, "strip", -1)
    order, inv, *stats = call(
        prepare, (offsets, images), [IN_SMEM, IN_VMEM], [jax.ShapeDtypeStruct((width, width), bf16)] + [tile_field] * 5,
        [IN_VMEM] * 6, [vmem(nv, height, LANES)] + [vmem(*field(kk))] * 2, 2**26, "prepare",
    )
    side_image, fwd_image = lax.optimization_barrier((side_image, fwd_image))
    side_maps = call(
        side, (offsets, side_image, order, inv, *stats), [IN_SMEM] + [IN_VMEM] * 7, two_maps, IN_VMEM,
        work + [maps_shape, vmem(8 + 3, kk, SUBS, LANES), maps_shape], 2**28, "side",
    )
    side_back = shifted(side_maps, "strip", 1)
    fwd_maps = call(
        forward, (offsets, fwd_image, order, inv, *stats), [IN_SMEM] + [IN_VMEM] * 7, two_maps, IN_VMEM,
        work + [vmem(nv, height, LANES), vmem(kk + 3, 8, SUBS, LANES), maps_shape], 2**28, "forward",
    )
    fwd_back = shifted(fwd_maps, "along", 1)
    out = call(
        functools.partial(collect, (0, 4, 6)), (fwd_maps, side_maps, side_back), [IN_VMEM] * 3, whole, IN_ANY,
        [pltpu.SemaphoreType.DMA((3,))], 2**20, "collect",
    )
    return call(
        functools.partial(collect, (2,)), (fwd_back, out), [IN_VMEM, IN_ANY], whole, IN_ANY,
        [pltpu.SemaphoreType.DMA((1,))], 2**20, "complete", {1: 0},
    )


def solution(mesh):
    return jax.shard_map(
        per_device, mesh=mesh, in_specs=(P("strip", "along"), P("strip", "along", None)),
        out_specs=P(None, "strip", "along"), check_vma=False,
    )
```

```python
import functools
import math

import jax
import jax.numpy as jnp
from jax import lax
from jax.experimental import pallas as pl
from jax.experimental.pallas import tpu as pltpu
from jax.sharding import PartitionSpec as P

DISP = 16
RADIUS = 4
LANES, SUBS = 128, 8
GROUP = 4
CENTRE = 128.0
VMEM_LIMIT = 24 * 2**20
f32, bf16, i32 = jnp.float32, jnp.bfloat16, jnp.int32
IN_VMEM = pl.BlockSpec(memory_space=pltpu.VMEM)
IN_SMEM = pl.BlockSpec(memory_space=pltpu.SMEM)
IN_ANY = pl.BlockSpec(memory_space=pl.ANY)


def iota(axis):
    return lax.broadcasted_iota(i32, (SUBS, LANES), axis)


def loop(n, body, unroll=True):
    lax.fori_loop(0, n, lambda i, c: (body(i), c)[1], 0, unroll=unroll)


def swap(x, n):
    return jnp.take_along_axis(x, iota(1) ^ n, axis=1, mode="promise_in_bounds")


def sums(x):
    front = [x[0]]
    for i in range(1, 8):
        front.append(front[-1] + x[i])
    back = [front[7]] + [x[7]] * 7
    for i in range(6, 0, -1):
        back[i] = back[i + 1] + x[i]
    return front, back


def box_cols(x):
    lane = iota(1)
    fa, ba = sums(x[:8])
    fb, bb = sums(x[8:])
    before = lambda y: jnp.where(lane >= GROUP, pltpu.roll(y, GROUP, 1), 0.0)
    after = lambda y: jnp.where(lane < LANES - GROUP, pltpu.roll(y, LANES - GROUP, 1), 0.0)
    out = [before(bb[k + 4]) + fa[k + 4] for k in range(4)]
    out += [ba[k] + fb[k] for k in range(8)]
    return out + [bb[k] + after(fa[k]) for k in range(4)]


def box_rows(x):
    sub = iota(0)
    front, back = sums(x)
    before = lambda y: jnp.where(sub >= 1, pltpu.roll(y, 1, 0), 0.0)
    after = lambda y: jnp.where(sub < SUBS - 1, pltpu.roll(y, SUBS - 1, 0), 0.0)
    return [before(back[j + 4]) + front[j + 4] for j in range(4)] + [back[j] + after(front[j]) for j in range(4)]


def make_order(order_ref):
    width = order_ref.shape[0]
    nv = width // LANES
    row = lax.broadcasted_iota(i32, (width, LANES), 0)
    lane = lax.broadcasted_iota(i32, (width, LANES), 1)
    for v in range(nv):
        order_ref[:, v * LANES:(v + 1) * LANES] = jnp.where(row == nv * lane + v, 1.0, 0.0).astype(bf16)


def reorder(x, order_ref, back=False):
    rows = x.shape[0]
    hi = x.astype(bf16)
    rest = x - hi.astype(f32)
    mid = rest.astype(bf16)
    low = (rest - mid.astype(f32)).astype(bf16)
    dims = (((1,), (1 if back else 0,)), ((), ()))
    y = lax.dot_general(jnp.concatenate([hi, mid, low]), order_ref[...], dims, preferred_element_type=f32)
    return (y[:rows] + y[rows:2 * rows]) + y[2 * rows:]


def put(ref, x):
    for v in range(ref.shape[0]):
        ref[v, :x.shape[0]] = x[:, v * LANES:(v + 1) * LANES]


def inverse_counts(inv_ref, scale_ref, height, width):
    lane, sub = iota(1), iota(0)
    kk = inv_ref.shape[1]
    count = lambda i, n: 1.0 / (jnp.minimum(i + RADIUS, n - 1) - jnp.maximum(i - RADIUS, 0) + 1).astype(f32)
    cols = [count(lane // GROUP * kk + k, width) for k in range(kk)]
    for j in range(8):
        row = count(sub * 8 + j, height)
        for k in range(kk):
            inv = row * cols[k]
            inv_ref[j, k] = inv
            scale_ref[j, k] = inv * (-4.0 * math.log2(math.e))


def guide_stats(v_ref, stats, inv_ref, p_ref, q_ref):
    g_ref, a1_ref, a2_ref, mean_ref = stats
    nv, kk = v_ref.shape[0], inv_ref.shape[1]
    first_lane = iota(1) // GROUP * GROUP

    def spread(h):
        for j in range(8):
            for v in range(nv):
                x = v_ref[v, pl.ds(j, SUBS, stride=8)]
                g_ref[j, nv * h + v] = jnp.take_along_axis(x, first_lane + h, axis=1, mode="promise_in_bounds")
    loop(GROUP, spread, 1)

    def first(j):
        g = [g_ref[j, k] for k in range(kk)]
        for k, y in enumerate(box_cols(g)):
            p_ref[j, k] = y
        for k, y in enumerate(box_cols([x * x for x in g])):
            q_ref[j, k] = y
    loop(8, first)

    def second(k):
        s1 = box_rows([p_ref[j, k] for j in range(8)])
        s2 = box_rows([q_ref[j, k] for j in range(8)])
        for j in range(8):
            inv = inv_ref[j, k]
            mean = s1[j] * inv
            a1 = inv / (s2[j] * inv - mean * mean + 50.0)
            a1_ref[j, k] = a1
            a2_ref[j, k] = a1 * mean
            mean_ref[j, k] = mean
    loop(kk, second)


def forward_partner(v_ref, y_ref, t):
    nv = v_ref.shape[0]

    def body(m):
        n = m + t
        a = lax.rem(LANES - lax.rem(lax.div(n, nv), LANES), LANES)
        for j in range(8):
            y_ref[m, j] = pltpu.roll(v_ref[lax.rem(n, nv), pl.ds(j, SUBS, stride=8)], a, 1)
    loop(y_ref.shape[0], body)


def side_partner(v2_ref, z_ref, t):
    nv, height = v2_ref.shape[0], (v2_ref.shape[1] - SUBS) // 2
    odd, upper = iota(1) % 2 == 1, iota(1) % GROUP >= 2

    def one(m):
        start = [lax.rem(m + t + GROUP * h, height) for h in range(GROUP)]
        for v in range(nv):
            x = [v2_ref[v, pl.ds(start[h], SUBS, stride=8)] for h in range(GROUP)]
            for n in (0, 2):
                z_ref[m, nv * n + v] = jnp.where(odd, swap(x[n + 1], 1), x[n])
                z_ref[m, nv * (n + 1) + v] = jnp.where(odd, x[n + 1], swap(x[n], 1))
    loop(z_ref.shape[0], one)

    def two(m):
        for v in range(nv):
            for n in (0, 1):
                x, y = z_ref[m, nv * n + v], z_ref[m, nv * (n + 2) + v]
                z_ref[m, nv * n + v] = jnp.where(upper, swap(y, 2), x)
                z_ref[m, nv * (n + 2) + v] = jnp.where(upper, y, swap(x, 2))
    loop(z_ref.shape[0], two)


def pair_maps(partner, stats, inv_ref, work, out_ref):
    g_ref, a1_ref, a2_ref, mean_ref, scale_ref = stats
    p2_ref, q2_ref, a2w_ref, b2_ref, score_ref = work
    kk = g_ref.shape[1]
    levels = DISP // GROUP

    def first(d, e, j):
        g = [g_ref[j, k] for k in range(kk)]
        cost = [jnp.abs(g[k] - partner(j, k, d)) for k in range(kk)]
        for k, y in enumerate(box_cols(cost)):
            p2_ref[e, j, k] = y
        for k, y in enumerate(box_cols([x * y for x, y in zip(g, cost)])):
            q2_ref[e, j, k] = y

    def second(e, k):
        p = box_rows([p2_ref[e, j, k] for j in range(8)])
        q = box_rows([q2_ref[e, j, k] for j in range(8)])
        ca = [q[j] * a1_ref[j, k] - p[j] * a2_ref[j, k] for j in range(8)]
        cb = [p[j] * inv_ref[j, k] - ca[j] * mean_ref[j, k] for j in range(8)]
        for j, y in enumerate(box_rows(ca)):
            a2w_ref[e, j, k] = y
        for j, y in enumerate(box_rows(cb)):
            b2_ref[e, j, k] = y

    def third(d, e, j):
        a = box_cols([a2w_ref[e, j, k] for k in range(kk)])
        b = box_cols([b2_ref[e, j, k] for k in range(kk)])
        for k in range(kk):
            score_ref[d, j, k] = (a[k] * g_ref[j, k] + b[k]) * scale_ref[j, k]

    def levels2(n):
        d = 2 * n
        loop(8, lambda j: first(d, 0, j))
        for i in range(8):
            first(d + 1, 1, i)
            second(0, 2 * i)
            second(0, 2 * i + 1)
        for i in range(8):
            third(d, 0, i)
            second(1, 2 * i)
            second(1, 2 * i + 1)
        loop(8, lambda j: third(d + 1, 1, j))
    loop(levels // 2, levels2, 1)

    p_ref, q_ref, a_ref, b_ref = p2_ref.at[0], q2_ref.at[0], a2w_ref.at[0], b2_ref.at[0]

    nv = kk // GROUP
    odd, upper = iota(1) % 2 == 1, iota(1) % GROUP >= 2
    lane_level = (iota(1) % GROUP * levels).astype(f32)

    def tops(j):
        for k in range(kk):
            top = functools.reduce(jnp.maximum, [score_ref[d, j, k] for d in range(levels)])
            top = jnp.maximum(top, swap(top, 1))
            b_ref[j, k] = jnp.maximum(top, swap(top, 2))
    loop(8, tops)

    def weights(j):
        for k in range(kk):
            w = [jnp.exp2(score_ref[d, j, k] - b_ref[j, k]) for d in range(levels)]
            s = w[-1]
            t = s
            for d in range(levels - 2, 0, -1):
                s = s + w[d]
                t = t + s
            s = s + w[0]
            p_ref[j, k] = s
            q_ref[j, k] = t + lane_level * s
            a_ref[j, k] = functools.reduce(jnp.add, [x * x for x in w])
    loop(8, weights, 2)

    def halves(j):
        for v in range(nv):
            for ref in (p_ref, q_ref, a_ref):
                x = [ref[j, nv * h + v] for h in range(GROUP)]
                for n in (0, 2):
                    ref[j, n // 2 * nv + v] = jnp.where(odd, x[n + 1], x[n]) + swap(jnp.where(odd, x[n], x[n + 1]), 1)
    loop(8, halves)

    height = (out_ref.shape[1] - SUBS) // 2

    def last(j):
        for v in range(nv):
            lo, hi = ([ref[j, n * nv + v] for ref in (p_ref, q_ref, a_ref)] for n in range(2))
            s, t, u = (jnp.where(upper, y, x) + swap(jnp.where(upper, x, y), 2) for x, y in zip(lo, hi))
            r = 1.0 / s
            out_ref[v, pl.ds(j, SUBS, stride=8)] = t * r
            out_ref[v, pl.ds(height + j, SUBS, stride=8)] = u * (r * r)
    loop(8, last)


def restore(out_ref, order_ref):
    rows = out_ref.shape[1] - SUBS
    return reorder(jnp.concatenate([out_ref[v, :rows] for v in range(out_ref.shape[0])], axis=1), order_ref, back=True)


def field(kk, *lead):
    return (*lead, 8, kk, SUBS, LANES)


def call(body, ins, in_specs, outs, out_specs, scratch, flops, name, aliases={}):
    return pl.pallas_call(
        body, in_specs=in_specs, out_specs=out_specs, out_shape=outs, scratch_shapes=scratch, name=name,
        input_output_aliases=aliases,
        compiler_params=pltpu.CompilerParams(vmem_limit_bytes=VMEM_LIMIT),
        cost_estimate=pl.CostEstimate(flops=flops, bytes_accessed=2**20, transcendentals=0),
    )(*ins)


def per_device(images, offsets):
    height, width = images.shape
    kk = width // LANES * GROUP
    nv = width // LANES
    assert height == 8 * SUBS and kk == DISP
    tile_field = jax.ShapeDtypeStruct(field(kk), f32)
    vmem = lambda *shape: pltpu.VMEM(shape, f32)
    work = [vmem(*field(kk, 2))] * 4 + [vmem(*field(kk, DISP // GROUP))]

    def shifted(value, axis, steps):
        n = lax.axis_size(axis)
        return lax.ppermute(value, axis, [(i, i + steps) for i in range(max(0, -steps), min(n, n - steps))])

    def prepare(base_ref, image_ref, order_ref, inv_ref, g_ref, a1_ref, a2_ref, mean_ref, scale_ref, v_ref, p_ref, q_ref):
        make_order(order_ref)
        inverse_counts(inv_ref, scale_ref, height, width)
        put(v_ref, reorder(image_ref[...] - CENTRE, order_ref))
        guide_stats(v_ref, (g_ref, a1_ref, a2_ref, mean_ref), inv_ref, p_ref, q_ref)

    def finish(maps_ref, order_ref, out_ref):
        maps = restore(maps_ref, order_ref)
        out_ref[0] = maps[:height]
        out_ref[1] = maps[height:]

    def side(base_ref, other_ref, order_ref, inv_ref, g_ref, a1_ref, a2_ref, mean_ref, scale_ref, out_ref, *scratch):
        *work_refs, v2_ref, z_ref, maps_ref = scratch
        x = reorder(other_ref[...] - CENTRE, order_ref)
        put(v2_ref, jnp.concatenate([x, x]))
        side_partner(v2_ref, z_ref, base_ref[0, 0, 1])
        pair_maps(lambda j, k, d: z_ref[j + d, k], (g_ref, a1_ref, a2_ref, mean_ref, scale_ref), inv_ref, work_refs, maps_ref)
        finish(maps_ref, order_ref, out_ref)

    def forward(base_ref, other_ref, order_ref, inv_ref, g_ref, a1_ref, a2_ref, mean_ref, scale_ref, out_ref, *scratch):
        *work_refs, v_ref, y_ref, maps_ref = scratch
        put(v_ref, reorder(other_ref[...] - CENTRE, order_ref))
        forward_partner(v_ref, y_ref, base_ref[0, 0, 0])
        pair_maps(lambda j, k, d: y_ref[k + d, j], (g_ref, a1_ref, a2_ref, mean_ref, scale_ref), inv_ref, work_refs, maps_ref)
        finish(maps_ref, order_ref, out_ref)

    def collect(rows, *refs):
        out_ref, sems = refs[-2:]
        copies = [pltpu.make_async_copy(refs[i], out_ref.at[row:row + 2], sems.at[i]) for i, row in enumerate(rows)]
        for copy in copies:
            copy.start()
        for copy in copies:
            copy.wait()

    maps_shape = vmem(nv, 2 * height + SUBS, LANES)
    image_shape = vmem(nv, height + SUBS, LANES)
    two_maps = jax.ShapeDtypeStruct((2, height, width), f32)
    whole = jax.ShapeDtypeStruct((8, height, width), f32)
    fwd_image = shifted(images, "along", -1)
    side_image = shifted(images, "strip", -1)
    order, inv, *stats = call(
        prepare, (offsets, images), [IN_SMEM, IN_VMEM], [jax.ShapeDtypeStruct((width, width), bf16)] + [tile_field] * 6,
        [IN_VMEM] * 7, [image_shape] + [vmem(*field(kk))] * 2, 2**26, "prepare",
    )
    side_image, fwd_image = lax.optimization_barrier((side_image, fwd_image))
    side_maps = call(
        side, (offsets, side_image, order, inv, *stats), [IN_SMEM] + [IN_VMEM] * 8, two_maps, IN_VMEM,
        work + [maps_shape, vmem(8 + 3, kk, SUBS, LANES), maps_shape], 2**28, "side",
    )
    side_back = shifted(side_maps, "strip", 1)
    fwd_maps = call(
        forward, (offsets, fwd_image, order, inv, *stats), [IN_SMEM] + [IN_VMEM] * 8, two_maps, IN_VMEM,
        work + [image_shape, vmem(kk + 3, 8, SUBS, LANES), maps_shape], 2**28, "forward",
    )
    fwd_back = shifted(fwd_maps, "along", 1)
    out = call(
        functools.partial(collect, (0, 4, 6)), (fwd_maps, side_maps, side_back), [IN_VMEM] * 3, whole, IN_ANY,
        [pltpu.SemaphoreType.DMA((3,))], 2**20, "collect",
    )
    return call(
        functools.partial(collect, (2,)), (fwd_back, out), [IN_VMEM, IN_ANY], whole, IN_ANY,
        [pltpu.SemaphoreType.DMA((1,))], 2**20, "complete", {1: 0},
    )


def solution(mesh):
    return jax.shard_map(
        per_device, mesh=mesh, in_specs=(P("strip", "along"), P("strip", "along", None)),
        out_specs=P(None, "strip", "along"), check_vma=False,
    )
```

```python
import functools
import math

import jax
import jax.numpy as jnp
from jax import lax
from jax.experimental import pallas as pl
from jax.experimental.pallas import tpu as pltpu
from jax.sharding import PartitionSpec as P

DISP = 16
RADIUS = 4
LANES, SUBS = 128, 8
GROUP = 4
CENTRE = 128.0
VMEM_LIMIT = 24 * 2**20
f32, bf16, i32 = jnp.float32, jnp.bfloat16, jnp.int32
IN_VMEM = pl.BlockSpec(memory_space=pltpu.VMEM)
IN_SMEM = pl.BlockSpec(memory_space=pltpu.SMEM)
IN_ANY = pl.BlockSpec(memory_space=pl.ANY)


def iota(axis):
    return lax.broadcasted_iota(i32, (SUBS, LANES), axis)


def loop(n, body, unroll=True):
    lax.fori_loop(0, n, lambda i, c: (body(i), c)[1], 0, unroll=unroll)


def swap(x, n):
    return jnp.take_along_axis(x, iota(1) ^ n, axis=1, mode="promise_in_bounds")


def sums(x):
    front = [x[0]]
    for i in range(1, 8):
        front.append(front[-1] + x[i])
    back = [front[7]] + [x[7]] * 7
    for i in range(6, 0, -1):
        back[i] = back[i + 1] + x[i]
    return front, back


def box_cols(x):
    lane = iota(1)
    fa, ba = sums(x[:8])
    fb, bb = sums(x[8:])
    before = lambda y: jnp.where(lane >= GROUP, pltpu.roll(y, GROUP, 1), 0.0)
    after = lambda y: jnp.where(lane < LANES - GROUP, pltpu.roll(y, LANES - GROUP, 1), 0.0)
    out = [before(bb[k + 4]) + fa[k + 4] for k in range(4)]
    out += [ba[k] + fb[k] for k in range(8)]
    return out + [bb[k] + after(fa[k]) for k in range(4)]


def box_rows(x):
    sub = iota(0)
    front, back = sums(x)
    before = lambda y: jnp.where(sub >= 1, pltpu.roll(y, 1, 0), 0.0)
    after = lambda y: jnp.where(sub < SUBS - 1, pltpu.roll(y, SUBS - 1, 0), 0.0)
    return [before(back[j + 4]) + front[j + 4] for j in range(4)] + [back[j] + after(front[j]) for j in range(4)]


def make_order(order_ref):
    width = order_ref.shape[0]
    nv = width // LANES
    row = lax.broadcasted_iota(i32, (width, LANES), 0)
    lane = lax.broadcasted_iota(i32, (width, LANES), 1)
    for v in range(nv):
        order_ref[:, v * LANES:(v + 1) * LANES] = jnp.where(row == nv * lane + v, 1.0, 0.0).astype(bf16)


def reorder(x, order_ref, back=False):
    rows = x.shape[0]
    hi = x.astype(bf16)
    rest = x - hi.astype(f32)
    mid = rest.astype(bf16)
    low = (rest - mid.astype(f32)).astype(bf16)
    dims = (((1,), (1 if back else 0,)), ((), ()))
    y = lax.dot_general(jnp.concatenate([hi, mid, low]), order_ref[...], dims, preferred_element_type=f32)
    return (y[:rows] + y[rows:2 * rows]) + y[2 * rows:]


def put(ref, x):
    for v in range(ref.shape[0]):
        ref[v, :x.shape[0]] = x[:, v * LANES:(v + 1) * LANES]


def inverse_counts(inv_ref, scale_ref, height, width):
    lane, sub = iota(1), iota(0)
    kk = inv_ref.shape[1]
    count = lambda i, n: 1.0 / (jnp.minimum(i + RADIUS, n - 1) - jnp.maximum(i - RADIUS, 0) + 1).astype(f32)
    cols = [count(lane // GROUP * kk + k, width) for k in range(kk)]
    for j in range(8):
        row = count(sub * 8 + j, height)
        for k in range(kk):
            inv = row * cols[k]
            inv_ref[j, k] = inv
            scale_ref[j, k] = inv * (-4.0 * math.log2(math.e))


def guide_stats(v_ref, stats, inv_ref, p_ref, q_ref):
    g_ref, a1_ref, a2_ref, mean_ref = stats
    nv, kk = v_ref.shape[0], inv_ref.shape[1]
    first_lane = iota(1) // GROUP * GROUP

    def spread(h):
        for j in range(8):
            for v in range(nv):
                x = v_ref[v, pl.ds(j, SUBS, stride=8)]
                g_ref[j, nv * h + v] = jnp.take_along_axis(x, first_lane + h, axis=1, mode="promise_in_bounds")
    loop(GROUP, spread, 1)

    def first(j):
        g = [g_ref[j, k] for k in range(kk)]
        for k, y in enumerate(box_cols(g)):
            p_ref[j, k] = y
        for k, y in enumerate(box_cols([x * x for x in g])):
            q_ref[j, k] = y
    loop(8, first)

    def second(k):
        s1 = box_rows([p_ref[j, k] for j in range(8)])
        s2 = box_rows([q_ref[j, k] for j in range(8)])
        for j in range(8):
            inv = inv_ref[j, k]
            mean = s1[j] * inv
            a1 = inv / (s2[j] * inv - mean * mean + 50.0)
            a1_ref[j, k] = a1
            a2_ref[j, k] = a1 * mean
            mean_ref[j, k] = mean
    loop(kk, second)


def forward_partner(v_ref, y_ref, t):
    nv = v_ref.shape[0]

    def body(m):
        n = m + t
        a = lax.rem(LANES - lax.rem(lax.div(n, nv), LANES), LANES)
        for j in range(8):
            y_ref[m, j] = pltpu.roll(v_ref[lax.rem(n, nv), pl.ds(j, SUBS, stride=8)], a, 1)
    loop(y_ref.shape[0], body)


def side_partner(v2_ref, z_ref, t):
    nv, height = v2_ref.shape[0], (v2_ref.shape[1] - SUBS) // 2
    odd, upper = iota(1) % 2 == 1, iota(1) % GROUP >= 2

    def one(m):
        start = [lax.rem(m + t + GROUP * h, height) for h in range(GROUP)]
        for v in range(nv):
            x = [v2_ref[v, pl.ds(start[h], SUBS, stride=8)] for h in range(GROUP)]
            for n in (0, 2):
                z_ref[m, nv * n + v] = jnp.where(odd, swap(x[n + 1], 1), x[n])
                z_ref[m, nv * (n + 1) + v] = jnp.where(odd, x[n + 1], swap(x[n], 1))
    loop(z_ref.shape[0], one)

    def two(m):
        for v in range(nv):
            for n in (0, 1):
                x, y = z_ref[m, nv * n + v], z_ref[m, nv * (n + 2) + v]
                z_ref[m, nv * n + v] = jnp.where(upper, swap(y, 2), x)
                z_ref[m, nv * (n + 2) + v] = jnp.where(upper, y, swap(x, 2))
    loop(z_ref.shape[0], two)


def pair_maps(partner, stats, inv_ref, work, out_ref):
    g_ref, a1_ref, a2_ref, mean_ref, scale_ref = stats
    p2_ref, q2_ref, a2w_ref, b2_ref, score_ref = work
    kk = g_ref.shape[1]
    levels = DISP // GROUP

    def first(d, e, j):
        g = [g_ref[j, k] for k in range(kk)]
        cost = [jnp.abs(g[k] - partner(j, k, d)) for k in range(kk)]
        for k, y in enumerate(box_cols(cost)):
            p2_ref[e, j, k] = y
        for k, y in enumerate(box_cols([x * y for x, y in zip(g, cost)])):
            q2_ref[e, j, k] = y

    def second(e, k):
        p = box_rows([p2_ref[e, j, k] for j in range(8)])
        q = box_rows([q2_ref[e, j, k] for j in range(8)])
        ca = [q[j] * a1_ref[j, k] - p[j] * a2_ref[j, k] for j in range(8)]
        cb = [p[j] * inv_ref[j, k] - ca[j] * mean_ref[j, k] for j in range(8)]
        for j, y in enumerate(box_rows(ca)):
            a2w_ref[e, j, k] = y
        for j, y in enumerate(box_rows(cb)):
            b2_ref[e, j, k] = y

    def third(d, e, j):
        a = box_cols([a2w_ref[e, j, k] for k in range(kk)])
        b = box_cols([b2_ref[e, j, k] for k in range(kk)])
        for k in range(kk):
            score_ref[d, j, k] = (a[k] * g_ref[j, k] + b[k]) * scale_ref[j, k]

    def levels2(n):
        d = 2 * n
        loop(8, lambda j: first(d, 0, j))
        for i in range(8):
            first(d + 1, 1, i)
            second(0, 2 * i)
            second(0, 2 * i + 1)
        for i in range(8):
            third(d, 0, i)
            second(1, 2 * i)
            second(1, 2 * i + 1)
        loop(8, lambda j: third(d + 1, 1, j))
    loop(levels // 2, levels2, 1)

    p_ref, q_ref, a_ref, b_ref = p2_ref.at[0], q2_ref.at[0], a2w_ref.at[0], b2_ref.at[0]

    nv = kk // GROUP
    odd, upper = iota(1) % 2 == 1, iota(1) % GROUP >= 2
    lane_level = (iota(1) % GROUP * levels).astype(f32)

    def tops(j):
        for k in range(kk):
            top = functools.reduce(jnp.maximum, [score_ref[d, j, k] for d in range(levels)])
            top = jnp.maximum(top, swap(top, 1))
            b_ref[j, k] = jnp.maximum(top, swap(top, 2))
    loop(8, tops)

    def weights(j):
        for k in range(kk):
            w = [jnp.exp2(score_ref[d, j, k] - b_ref[j, k]) for d in range(levels)]
            s = w[-1]
            t = s
            for d in range(levels - 2, 0, -1):
                s = s + w[d]
                t = t + s
            s = s + w[0]
            p_ref[j, k] = s
            q_ref[j, k] = t + lane_level * s
            a_ref[j, k] = functools.reduce(jnp.add, [x * x for x in w])
    loop(8, weights, 2)

    def halves(j):
        for v in range(nv):
            for ref in (p_ref, q_ref, a_ref):
                x = [ref[j, nv * h + v] for h in range(GROUP)]
                for n in (0, 2):
                    ref[j, n // 2 * nv + v] = jnp.where(odd, x[n + 1], x[n]) + swap(jnp.where(odd, x[n], x[n + 1]), 1)
    loop(8, halves)

    height = (out_ref.shape[1] - SUBS) // 2

    def last(j):
        for v in range(nv):
            lo, hi = ([ref[j, n * nv + v] for ref in (p_ref, q_ref, a_ref)] for n in range(2))
            s, t, u = (jnp.where(upper, y, x) + swap(jnp.where(upper, x, y), 2) for x, y in zip(lo, hi))
            r = 1.0 / s
            out_ref[v, pl.ds(j, SUBS, stride=8)] = t * r
            out_ref[v, pl.ds(height + j, SUBS, stride=8)] = u * (r * r)
    loop(8, last)


def restore(out_ref, order_ref):
    rows = out_ref.shape[1] - SUBS
    return reorder(jnp.concatenate([out_ref[v, :rows] for v in range(out_ref.shape[0])], axis=1), order_ref, back=True)


def field(kk, *lead):
    return (*lead, 8, kk, SUBS, LANES)


def call(body, ins, in_specs, outs, out_specs, scratch, flops, name, aliases={}):
    return pl.pallas_call(
        body, in_specs=in_specs, out_specs=out_specs, out_shape=outs, scratch_shapes=scratch, name=name,
        input_output_aliases=aliases,
        compiler_params=pltpu.CompilerParams(vmem_limit_bytes=VMEM_LIMIT),
        cost_estimate=pl.CostEstimate(flops=flops, bytes_accessed=2**20, transcendentals=0),
    )(*ins)


def per_device(images, offsets):
    height, width = images.shape
    kk = width // LANES * GROUP
    nv = width // LANES
    assert height == 8 * SUBS and kk == DISP
    tile_field = jax.ShapeDtypeStruct(field(kk), f32)
    vmem = lambda *shape: pltpu.VMEM(shape, f32)
    work = [vmem(*field(kk, 2))] * 4 + [vmem(*field(kk, DISP // GROUP))]

    def shifted(value, axis, steps):
        n = lax.axis_size(axis)
        return lax.ppermute(value, axis, [(i, i + steps) for i in range(max(0, -steps), min(n, n - steps))])

    def prepare(base_ref, image_ref, order_ref, inv_ref, g_ref, a1_ref, a2_ref, mean_ref, scale_ref, v_ref, p_ref, q_ref):
        make_order(order_ref)
        inverse_counts(inv_ref, scale_ref, height, width)
        put(v_ref, reorder(image_ref[...] - CENTRE, order_ref))
        guide_stats(v_ref, (g_ref, a1_ref, a2_ref, mean_ref), inv_ref, p_ref, q_ref)

    def finish(maps_ref, order_ref, out_ref):
        maps = restore(maps_ref, order_ref)
        out_ref[0] = maps[:height]
        out_ref[1] = maps[height:]

    def side(base_in, other_ref, order_ref, inv_ref, g_ref, a1_ref, a2_ref, mean_ref, scale_ref, out_ref, *scratch):
        *work_refs, v2_ref, z_ref, maps_ref, base_ref, sem = scratch
        copy = pltpu.make_async_copy(base_in, base_ref, sem)
        copy.start()
        x = reorder(other_ref[...] - CENTRE, order_ref)
        put(v2_ref, jnp.concatenate([x, x]))
        copy.wait()
        side_partner(v2_ref, z_ref, base_ref[0, 0, 1])
        pair_maps(lambda j, k, d: z_ref[j + d, k], (g_ref, a1_ref, a2_ref, mean_ref, scale_ref), inv_ref, work_refs, maps_ref)
        finish(maps_ref, order_ref, out_ref)

    def forward(base_in, other_ref, order_ref, inv_ref, g_ref, a1_ref, a2_ref, mean_ref, scale_ref, out_ref, *scratch):
        *work_refs, v_ref, y_ref, maps_ref, base_ref, sem = scratch
        copy = pltpu.make_async_copy(base_in, base_ref, sem)
        copy.start()
        put(v_ref, reorder(other_ref[...] - CENTRE, order_ref))
        copy.wait()
        forward_partner(v_ref, y_ref, base_ref[0, 0, 0])
        pair_maps(lambda j, k, d: y_ref[k + d, j], (g_ref, a1_ref, a2_ref, mean_ref, scale_ref), inv_ref, work_refs, maps_ref)
        finish(maps_ref, order_ref, out_ref)

    def collect(rows, *refs):
        out_ref, sems = refs[-2:]
        copies = [pltpu.make_async_copy(refs[i], out_ref.at[row:row + 2], sems.at[i]) for i, row in enumerate(rows)]
        for copy in copies:
            copy.start()
        for copy in copies:
            copy.wait()

    maps_shape = vmem(nv, 2 * height + SUBS, LANES)
    base_scratch = [pltpu.SMEM(offsets.shape, i32), pltpu.SemaphoreType.DMA]
    image_shape = vmem(nv, height + SUBS, LANES)
    two_maps = jax.ShapeDtypeStruct((2, height, width), f32)
    whole = jax.ShapeDtypeStruct((8, height, width), f32)
    fwd_image = shifted(images, "along", -1)
    side_image = shifted(images, "strip", -1)
    order, inv, *stats = call(
        prepare, (offsets, images), [IN_SMEM, IN_VMEM], [jax.ShapeDtypeStruct((width, width), bf16)] + [tile_field] * 6,
        [IN_VMEM] * 7, [image_shape] + [vmem(*field(kk))] * 2, 2**26, "prepare",
    )
    side_image, fwd_image = lax.optimization_barrier((side_image, fwd_image))
    side_maps = call(
        side, (offsets, side_image, order, inv, *stats), [IN_VMEM] * 9, two_maps, IN_VMEM,
        work + [maps_shape, vmem(8 + 3, kk, SUBS, LANES), maps_shape] + base_scratch, 2**28, "side",
    )
    side_back = shifted(side_maps, "strip", 1)
    fwd_maps = call(
        forward, (offsets, fwd_image, order, inv, *stats), [IN_VMEM] * 9, two_maps, IN_VMEM,
        work + [image_shape, vmem(kk + 3, 8, SUBS, LANES), maps_shape] + base_scratch, 2**28, "forward",
    )
    fwd_back = shifted(fwd_maps, "along", 1)
    out = call(
        functools.partial(collect, (0, 4, 6)), (fwd_maps, side_maps, side_back), [IN_VMEM] * 3, whole, IN_ANY,
        [pltpu.SemaphoreType.DMA((3,))], 2**20, "collect",
    )
    return call(
        functools.partial(collect, (2,)), (fwd_back, out), [IN_VMEM, IN_ANY], whole, IN_ANY,
        [pltpu.SemaphoreType.DMA((1,))], 2**20, "complete", {1: 0},
    )


def solution(mesh):
    return jax.shard_map(
        per_device, mesh=mesh, in_specs=(P("strip", "along"), P("strip", "along", None)),
        out_specs=P(None, "strip", "along"), check_vma=False,
    )
```
